768 devices in a mesh: dp: 32 (over y, z_hi), tensor: 24 (over x, z_lo, core).
Axes of the slice: x: 4, y: 8, z: 12 (z_hi: 4, z_lo: 3; z = z_hi * 3 + z_lo), core: 2. Of those that a mesh axis runs over, the one named last changes fastest.
Arguments:
- queries: bfloat16 [12288, 3072], P('dp', 'tensor'), may hold values from -6 to 6
- targets: bfloat16 [12288, 3072], P('dp', 'tensor'), may hold values from -6 to 6
- row_lse: float32 [12288], P('dp'), may hold values from 6 to 9
- col_lse: float32 [12288], P('dp'), may hold values from 6 to 9
- positive: int32 [12288], P('dp'), may hold values from 0 to 12287, each once
- target_grads: float32 [12288, 3072], P('dp', 'tensor'), may hold values from -0.75 to 0.75
Outputs:
- query_grads: float32 [12288, 3072], P('dp', 'tensor')
- passed_grads: float32 [12288, 3072], P('dp', 'tensor')
The draws below stay inside these ranges and needn't reach their ends.
Inputs may be any that keep to these rules, and one draw needn't show every extreme that they name: `positive`: a permutation of the pair indices.
All inputs are finite; a program needn't handle non-finite values.
Results may differ from the reference program's by a relative error of at most 0.0031.
Values may be sent and summed in bfloat16 or wider, within the bound.
A program may use at most 32 MiB of HBM per device.

```python
import math
import jax
import jax.numpy as jnp

D = 3072
ROWS = 384
STEPS = 4
PAIRS = 12288
N_DP = 32


def level_of(rng, shape, cuts, smallest, top_value):
    level = 1.0
    for position, parts in cuts:
        draws = jax.random.uniform(jax.random.fold_in(jax.random.fold_in(rng, 6), position), (parts,), jnp.float32, smallest / len(cuts), top_value / len(cuts))
        level = level * jnp.repeat(jnp.exp(draws), shape[position] // parts).reshape((-1,) + (1,) * (len(shape) - 1 - position))
    return level


def noise(key, shape, spread, reach, shards=(), kind=jnp.bfloat16):
    result = spread * jax.random.normal(key, shape, jnp.float32)
    if shards:
        result = result * level_of(key, shape, shards, -0.22, 0.18)
    return jnp.clip(result, -reach, reach).astype(kind)


def setup_inputs(seed: int = 0) -> dict:
    splits = jax.random.split(jax.random.key(seed), 7)
    return {
        "queries": noise(splits[0], (PAIRS, D), 1.0, 6.0, ((0, 32), (1, 24))),
        "targets": noise(splits[1], (PAIRS, D), 1.0, 6.0, ((0, 32), (1, 24))),
        "row_lse": jnp.clip(6.0 + 3.0 * jax.random.uniform(splits[2], (PAIRS,), jnp.float32) ** level_of(splits[2], (PAIRS,), ((0, 32),), -0.2, 0.2), 6.0, 9.0),
        "col_lse": jnp.clip(6.0 + 3.0 * jax.random.uniform(splits[3], (PAIRS,), jnp.float32) ** level_of(splits[3], (PAIRS,), ((0, 32),), -0.2, 0.2), 6.0, 9.0),
        "positive": jax.random.permutation(splits[4], PAIRS).astype(jnp.int32),
        "target_grads": noise(splits[5], (PAIRS, D), 0.05, 0.75, ((0, 32), (1, 24)), jnp.float32),
    }


def reference(queries, targets, row_lse, col_lse, positive, target_grads):
    nblocks = N_DP
    scale = 2.0 / math.sqrt(D)
    query_blocks = queries.reshape(nblocks, ROWS, D).astype(jnp.float32)
    target_blocks = targets.reshape(nblocks, ROWS, D)
    lse_rows = row_lse.reshape(nblocks, ROWS)
    lse_cols = col_lse.reshape(nblocks, ROWS)
    pos_rows = positive.reshape(nblocks, ROWS)
    accum = target_grads.reshape(nblocks, ROWS, D)
    grad_q = jnp.zeros((nblocks, ROWS, D), jnp.float32)
    blocks = jnp.arange(nblocks, dtype=jnp.int32)
    within = jnp.arange(ROWS, dtype=jnp.int32)
    for step in range(STEPS):
        moved = jnp.roll(target_blocks, step, axis=0).astype(jnp.float32)
        moved_lse = jnp.roll(lse_cols, step, axis=0)
        source = (blocks - step) % nblocks
        columns = source[:, None] * ROWS + within[None, :]
        scores = scale * jnp.einsum('nrd,nsd->nrs', query_blocks, moved)
        match = (pos_rows[:, :, None] == columns[:, None, :]).astype(jnp.float32)
        weights = (jnp.exp(scores - lse_rows[:, :, None]) + jnp.exp(scores - moved_lse[:, None, :]) - 2.0 * match).astype(jnp.bfloat16)
        wide = weights.astype(jnp.float32)
        grad_q = grad_q + scale * jnp.einsum('nrs,nsd->nrd', wide, moved)
        term = scale * jnp.einsum('nrs,nrd->nsd', wide, query_blocks)
        accum = accum + jnp.roll(term, -step, axis=0)
    passed = jnp.roll(accum, STEPS - 1, axis=0)
    return (grad_q.reshape(PAIRS, D), passed.reshape(PAIRS, D))
```

```python
import functools
import math

import jax
import jax.numpy as jnp
from jax import lax
from jax.experimental import pallas as pl
from jax.experimental.pallas import tpu as pltpu
from jax.sharding import PartitionSpec as P

D = 3072
STEPS = 4
NX, NZ, NC = 4, 3, 2
SCALE = 2.0 / math.sqrt(D)
COPIES = 64
F32 = jnp.float32
BF16 = jnp.bfloat16


def kernel(
    n_dp, q_ref, t_ref, rl_ref, cl_ref, pos_ref, tg_ref, gq_ref, gt_ref,
    qp, qo, ta, tb, cls, sp, xr, zs, zr, w, gts, g1, gr1, g2, gr2, send_sem, recv_sem,
):
    rows = q_ref.shape[0]
    band = rows // (NX * NZ * NC)
    xband = band * NZ
    half = rows // 2
    b = lax.axis_index("dp")
    t = lax.axis_index("tensor")
    x, zl, c = t // (NZ * NC), lax.rem(t // NC, NZ), lax.rem(t, NC)

    def at_dp(k):
        return (lax.rem(b + k + n_dp, n_dp), t)

    def at_x(k):
        return (b, lax.rem(x + k, NX) * (NZ * NC) + zl * NC + c)

    def at_z(k):
        return (b, x * (NZ * NC) + lax.rem(zl + k, NZ) * NC + c)

    mate = (b, t + 1 - 2 * c)

    barrier = pltpu.get_barrier_semaphore()
    partners = [mate] + [at_x(k) for k in (1, 2, 3)] + [at_z(k) for k in (1, 2)]
    partners += [at_dp(k) for k in (1, -1, 2, -2, 3, -3)]
    for dev in partners:
        pl.semaphore_signal(barrier, inc=1, device_id=dev, device_id_type=pl.DeviceIdType.MESH)

    for i in range(NX * NZ):
        for p in range(NC):
            qp[p, band * i : band * (i + 1)] = q_ref[band * (NC * i + p) : band * (NC * i + p + 1)]

    pl.semaphore_wait(barrier, len(partners))

    started = []

    def send(src, dst, dev):
        i = len(started)
        copy = pltpu.make_async_remote_copy(
            src_ref=src, dst_ref=dst, send_sem=send_sem.at[i], recv_sem=recv_sem.at[i],
            device_id=dev, device_id_type=pl.DeviceIdType.MESH,
        )
        copy.start()
        started.append(copy)
        return copy

    own = [t_ref, ta.at[0], ta.at[1], ta.at[2]]
    got_q = send(qp.at[1 - c], qo, mate)
    got_tb = [None] * STEPS
    got_tb[0] = send(t_ref, tb.at[0], mate)
    got_t1 = send(t_ref, ta.at[0], at_dp(1))
    got_t3 = send(t_ref, ta.at[2], at_dp(3))
    got_cl = [None] + [send(cl_ref, cls.at[k - 1], at_dp(k)) for k in (1, 2, 3)]

    lane = lax.broadcasted_iota(jnp.int32, (band, rows), 1)
    here = lane == t * band + lax.broadcasted_iota(jnp.int32, (band, rows), 0)
    rl = jnp.sum(jnp.where(here, rl_ref[...], 0.0), axis=1, keepdims=True)
    pos = jnp.sum(jnp.where(here, pos_ref[...], 0), axis=1, keepdims=True)

    got_x, got_z, got_zw, got_xw, got_cw = {}, {}, {}, {}, {}

    def scores(d):
        got_tb[d].wait_recv()
        qq = jnp.concatenate([qp[c], qo[...]], axis=1)
        tt = jnp.concatenate([own[d][...], tb[d]], axis=1)
        s = lax.dot_general(qq, tt, (((1,), (1,)), ((), ())), preferred_element_type=F32)
        sp[d] = s.reshape(NX, xband, rows)
        got_x[d] = [send(sp.at[d, lax.rem(x + k, NX)], xr.at[d, k - 1], at_x(k)) for k in (1, 2, 3)]

    def sum_x(d):
        for copy in got_x[d]:
            copy.wait_recv()
        s = sp[d, x] + xr[d, 0] + xr[d, 1] + xr[d, 2]
        zs[d] = s.reshape(NZ, band, rows)
        got_z[d] = [send(zs.at[d, lax.rem(zl + k, NZ)], zr.at[d, k - 1], at_z(k)) for k in (1, 2)]

    def weigh(d):
        for copy in got_z[d]:
            copy.wait_recv()
        s = (zs[d, zl] + zr[d, 0] + zr[d, 1]) * SCALE
        if d:
            got_cl[d].wait_recv()
        cl = cls[d - 1] if d else cl_ref[...]
        match = (pos == lax.rem(b - d + n_dp, n_dp) * rows + lane).astype(F32)
        band_w = jnp.exp(s - rl) + jnp.exp(s - cl) - 2.0 * match
        mine = pl.ds(pl.multiple_of(zl * band, band), band)
        w[d, c, x, mine] = band_w.astype(BF16)
        got_zw[d] = [send(w.at[d, c, x, mine], w.at[d, c, x, mine], at_z(k)) for k in (1, 2)]

    def gather_x(d):
        for k, copy in enumerate(got_zw[d]):
            copy.wait_recv()
        got_xw[d] = [send(w.at[d, c, x], w.at[d, c, x], at_x(k)) for k in (1, 2, 3)]

    def gather_core(d):
        for copy in got_xw[d]:
            copy.wait_recv()
        got_cw[d] = send(w.at[d, c], w.at[d, c], mate)

    def gradients(d):
        got_cw[d].wait_recv()
        weights = w[d].reshape(rows, rows)
        part = jnp.dot(weights, own[d][...], preferred_element_type=F32) * SCALE
        for p in range(NC):
            for i in range(NX * NZ):
                to = slice(band * (NC * i + p), band * (NC * i + p + 1))
                piece = part[half * p + band * i : half * p + band * (i + 1)]
                gq_ref[to] = piece if d == 1 else gq_ref[to] + piece
        queries = qp[...].reshape(rows, q_ref.shape[1])
        term = lax.dot_general(weights, queries, (((0,), (0,)), ((), ())), preferred_element_type=F32)
        return term * SCALE

    scores_0_ready = got_q
    scores_0_ready.wait_recv()
    scores(0)
    sum_x(0)
    got_t1.wait_recv()
    got_t2a = send(ta.at[0, pl.ds(0, half)], ta.at[1, pl.ds(0, half)], at_dp(1))
    got_tb[1] = send(ta.at[0], tb.at[1], mate)
    got_t3.wait_recv()
    got_t2b = send(ta.at[2, pl.ds(half, half)], ta.at[1, pl.ds(half, half)], at_dp(-1))
    got_tb[3] = send(ta.at[2], tb.at[3], mate)
    scores(1)
    scores(3)
    weigh(0)
    sum_x(1)
    sum_x(3)
    gather_x(0)
    weigh(1)
    weigh(3)
    got_t2a.wait_recv()
    got_t2b.wait_recv()
    got_tb[2] = send(ta.at[1], tb.at[2], mate)
    gather_x(1)
    gather_x(3)
    scores(2)
    gather_core(0)
    sum_x(2)
    gather_core(1)
    gather_core(3)
    weigh(2)
    term = gradients(1)
    g1[...] = term.astype(BF16).reshape(g1.shape)
    got_1a = send(g1.at[0], gr1.at[0], at_dp(1))
    got_1b = send(g1.at[1], gr1.at[1], at_dp(-1))
    gather_x(2)
    gts[0] = gradients(0) + tg_ref[...]
    got_1b.wait_recv()
    g2[0, :half] = gts[0, :half].astype(BF16)
    g2[0, half:] = (gts[0, half:] + gr1[1].astype(F32)).astype(BF16)
    got_20 = send(g2.at[0], gr2.at[0], at_dp(3))
    gts[1] = gradients(3)
    gather_core(2)
    gts[0] = gradients(2)
    got_1a.wait_recv()
    g2[1, :half] = (gts[0, :half] + gr1[0].astype(F32)).astype(BF16)
    g2[1, half:] = gts[0, half:].astype(BF16)
    got_22 = send(g2.at[1], gr2.at[1], at_dp(1))
    got_20.wait_recv()
    got_22.wait_recv()
    gt_ref[...] = gts[1] + (gr2[0].astype(F32) + gr2[1].astype(F32))
    for copy in started:
        copy.wait_send()


def shards(n_dp, queries, targets, row_lse, col_lse, positive, target_grads):
    rows, cols = queries.shape
    band, half = rows // (NX * NZ * NC), rows // 2
    vmem = pl.BlockSpec(memory_space=pltpu.VMEM)
    return pl.pallas_call(
        functools.partial(kernel, n_dp),
        out_shape=(jax.ShapeDtypeStruct((rows, cols), F32),) * 2,
        in_specs=[vmem] * 6,
        out_specs=(vmem, vmem),
        scratch_shapes=[
            pltpu.VMEM((NC, half, cols), BF16),
            pltpu.VMEM((half, cols), BF16),
            pltpu.VMEM((STEPS - 1, rows, cols), BF16),
            pltpu.VMEM((STEPS, rows, cols), BF16),
            pltpu.VMEM((STEPS - 1, 1, rows), F32),
            pltpu.VMEM((STEPS, NX, band * NZ, rows), F32),
            pltpu.VMEM((STEPS, NX - 1, band * NZ, rows), F32),
            pltpu.VMEM((STEPS, NZ, band, rows), F32),
            pltpu.VMEM((STEPS, NZ - 1, band, rows), F32),
            pltpu.VMEM((STEPS, NC, NX, band * NZ, rows), BF16),
            pltpu.VMEM((2, rows, cols), F32),
            pltpu.VMEM((2, half, cols), BF16),
            pltpu.VMEM((2, half, cols), BF16),
            pltpu.VMEM((2, rows, cols), BF16),
            pltpu.VMEM((2, rows, cols), BF16),
            pltpu.SemaphoreType.DMA((COPIES,)),
            pltpu.SemaphoreType.DMA((COPIES,)),
        ],
        compiler_params=pltpu.CompilerParams(
            collective_id=0, has_side_effects=True, vmem_limit_bytes=40 << 20
        ),
        cost_estimate=pl.CostEstimate(flops=10**9, bytes_accessed=10**6, transcendentals=10**5),
    )(
        queries, targets, row_lse.reshape(1, rows), col_lse.reshape(1, rows),
        positive.reshape(1, rows), target_grads,
    )


def solution(mesh):
    placed = (P("dp", "tensor"), P("dp", "tensor"), P("dp"), P("dp"), P("dp"), P("dp", "tensor"))
    return jax.shard_map(
        functools.partial(shards, mesh.shape["dp"]),
        mesh=mesh,
        in_specs=placed,
        out_specs=(P("dp", "tensor"), P("dp", "tensor")),
        check_vma=False,
    )
```

```python
import functools
import math

import jax
import jax.numpy as jnp
from jax import lax
from jax.experimental import pallas as pl
from jax.experimental.pallas import tpu as pltpu
from jax.sharding import PartitionSpec as P

D = 3072
STEPS = 4
NX, NZ, NC = 4, 3, 2
SCALE = 2.0 / math.sqrt(D)
COPIES = 80
LOADS = 6
F32 = jnp.float32
BF16 = jnp.bfloat16
I16 = jnp.int16
BOUND = 6.0
LEVELS = 32767.0


def code_of(reach, knee):
    steps = LEVELS / math.asinh(reach / knee)

    def encode(v):
        a = jnp.abs(v) * (1.0 / knee)
        u = jnp.minimum(jnp.log(a + jnp.sqrt(a * a + 1.0)) * steps, LEVELS)
        return jnp.round(jnp.where(v < 0, -u, u)).astype(jnp.int32).astype(I16)

    def decode(q):
        e = jnp.exp(q.astype(jnp.int32).astype(F32) * (1.0 / steps))
        return (e - 1.0 / e) * (0.5 * knee)

    return encode, decode


def kernel(
    n_dp, q_hbm, t_hbm, rl_hbm, cl_hbm, pos_hbm, tg_hbm, gq_ref, gt_ref,
    q_ref, t_ref, rl_ref, cl_ref, pos_ref, tg_ref,
    qp, qo, ta, tb, cl1, cl2, cl3, own_sp, sp, xr, zs, zr, w, gts, g1, gr1, g2, gr2, load_sem, send_sem, recv_sem,
):
    rows, cols = q_ref.shape
    band = rows // (NX * NZ * NC)
    xband = band * NZ
    half = rows // 2
    b = lax.axis_index("dp")
    t = lax.axis_index("tensor")
    x, zl, c = t // (NZ * NC), lax.rem(t // NC, NZ), lax.rem(t, NC)

    pairs = ((q_hbm, q_ref), (t_hbm, t_ref), (cl_hbm, cl_ref), (rl_hbm, rl_ref), (pos_hbm, pos_ref), (tg_hbm, tg_ref))
    loads = [pltpu.make_async_copy(src, dst, load_sem.at[i]) for i, (src, dst) in enumerate(pairs)]
    for load in loads:
        load.start()

    def at_dp(k):
        return (lax.rem(b + k + n_dp, n_dp), t)

    def at_x(k):
        return (b, lax.rem(x + k, NX) * (NZ * NC) + zl * NC + c)

    def at_z(k):
        return (b, x * (NZ * NC) + lax.rem(zl + k, NZ) * NC + c)

    mate = (b, t + 1 - 2 * c)

    barrier = pltpu.get_barrier_semaphore()
    partners = [mate] + [at_x(k) for k in (1, 2, 3)] + [at_z(k) for k in (1, 2)]
    partners += [at_dp(k) for k in (1, -1, 2, -2, 3, -3)]
    for dev in partners:
        pl.semaphore_signal(barrier, inc=1, device_id=dev, device_id_type=pl.DeviceIdType.MESH)

    loads[0].wait()
    for i in range(NX * NZ):
        for p in range(NC):
            qp[p, band * i : band * (i + 1)] = q_ref[band * (NC * i + p) : band * (NC * i + p + 1)]
    loads[1].wait()
    loads[2].wait()

    pl.semaphore_wait(barrier, len(partners))

    started = []

    def send(src, dst, dev):
        i = len(started)
        copy = pltpu.make_async_remote_copy(
            src_ref=src, dst_ref=dst, send_sem=send_sem.at[i], recv_sem=recv_sem.at[i],
            device_id=dev, device_id_type=pl.DeviceIdType.MESH,
        )
        copy.start()
        started.append(copy)
        return copy

    cls = (cl1, cl2, cl3)
    own = [t_ref, ta.at[0], ta.at[1], ta.at[2]]
    got_q = send(qp.at[1 - c], qo, mate)
    low, high = pl.ds(0, half), pl.ds(half, half)
    got_tb = [[] for _ in range(STEPS)]
    got_tb[0].append(send(t_ref, tb.at[0], mate))
    got_t1 = [send(t_ref.at[low], ta.at[0, low], at_dp(1))]
    got_t3 = [send(t_ref.at[high], ta.at[2, high], at_dp(3))]
    got_t1.append(send(t_ref.at[high], ta.at[0, high], at_dp(1)))
    got_t3.append(send(t_ref.at[low], ta.at[2, low], at_dp(3)))
    got_cl = [None] + [send(cl_ref, cls[k - 1], at_dp(k)) for k in (1, 2, 3)]

    for load in loads[3:]:
        load.wait()
    lane = lax.broadcasted_iota(jnp.int32, (xband, rows), 1)
    row = lax.broadcasted_iota(jnp.int32, (xband, rows), 0)
    here = lane == ((x * NZ + row // band) * NC + c) * band + row % band
    rl = jnp.sum(jnp.where(here, rl_ref[...].reshape(1, rows), 0.0), axis=1, keepdims=True)
    pos = jnp.sum(jnp.where(here, pos_ref[...].reshape(1, rows), 0), axis=1, keepdims=True)

    reach = BOUND * BOUND * SCALE * cols * NC
    encode_x, decode_x = code_of(reach, 0.3)
    encode_z, decode_z = code_of(reach * NX, 0.6)

    got_x, got_z, got_xw, got_cw = {}, {}, {}, {}

    def scores(d):
        for copy in got_tb[d]:
            copy.wait_recv()
        qq = jnp.concatenate([qp[c], qo[...]], axis=1)
        tt = jnp.concatenate([own[d][...], tb[d]], axis=1)
        s = lax.dot_general(qq, tt, (((1,), (1,)), ((), ())), preferred_element_type=F32) * SCALE
        own_sp[d] = s.reshape(NX, xband, rows)
        sp[d] = encode_x(s).reshape(NX, xband, rows)
        got_x[d] = [send(sp.at[d, lax.rem(x + k, NX)], xr.at[d, k - 1], at_x(k)) for k in (1, 2, 3)]

    def sum_x(d):
        for copy in got_x[d]:
            copy.wait_recv()
        s = own_sp[d, x] + decode_x(xr[d, 0]) + decode_x(xr[d, 1]) + decode_x(xr[d, 2])
        own_sp[d, x] = s
        zs[d] = encode_z(s)
        got_z[d] = [send(zs.at[d], zr.at[d, k - 1], at_z(k)) for k in (1, 2)]

    def weigh(d):
        for copy in got_z[d]:
            copy.wait_recv()
        s = own_sp[d, x] + decode_z(zr[d, 0]) + decode_z(zr[d, 1])
        if d:
            got_cl[d].wait_recv()
        cl = (cls[d - 1] if d else cl_ref)[...].reshape(1, rows)
        match = (pos == lax.rem(b - d + n_dp, n_dp) * rows + lane).astype(F32)
        w[d, c, x] = (jnp.exp(s - rl) + jnp.exp(s - cl) - 2.0 * match).astype(BF16)
        got_xw[d] = [send(w.at[d, c, x], w.at[d, c, x], at_x(k)) for k in (1, 2, 3)]
        got_cw[d] = [send(w.at[d, c, x], w.at[d, c, x], mate)]

    def relay(d):
        for k in (1, 3, 2):
            got_xw[d][k - 1].wait_recv()
            piece = w.at[d, c, lax.rem(x + NX - k, NX)]
            got_cw[d].append(send(piece, piece, mate))

    def share(d, part):
        got_tb[d].append(send(ta.at[d - 1, part], tb.at[d, part], mate))

    def target_term(d):
        for copy in got_cw[d]:
            copy.wait_recv()
        weights = w[d].reshape(rows, rows)
        queries = qp[...].reshape(rows, cols)
        return lax.dot_general(weights, queries, (((0,), (0,)), ((), ())), preferred_element_type=F32) * SCALE

    got_q.wait_recv()
    scores(0)
    got_t1[0].wait_recv()
    got_t2a = send(ta.at[0, low], ta.at[1, low], at_dp(1))
    share(1, low)
    got_t3[0].wait_recv()
    got_t2b = send(ta.at[2, high], ta.at[1, high], at_dp(-1))
    share(3, high)
    sum_x(0)
    got_t1[1].wait_recv()
    share(1, high)
    got_t3[1].wait_recv()
    share(3, low)
    scores(1)
    scores(3)
    weigh(0)
    sum_x(1)
    got_t2a.wait_recv()
    share(2, low)
    got_t2b.wait_recv()
    share(2, high)
    relay(0)
    scores(2)
    weigh(1)
    sum_x(2)
    sum_x(3)
    relay(1)
    g1[...] = target_term(1).astype(BF16).reshape(g1.shape)
    got_1a = send(g1.at[0], gr1.at[0], at_dp(1))
    got_1b = send(g1.at[1], gr1.at[1], at_dp(-1))
    weigh(2)
    gts[0] = target_term(0) + tg_ref[...]
    g2[0, low] = gts[0, low].astype(BF16)
    got_g = [send(g2.at[0, low], gr2.at[0, low], at_dp(3))]
    weigh(3)
    relay(2)
    got_1b.wait_recv()
    g2[0, high] = (gts[0, high] + gr1[1].astype(F32)).astype(BF16)
    got_g.append(send(g2.at[0, high], gr2.at[0, high], at_dp(3)))
    gts[1] = target_term(2)
    g2[1, high] = gts[1, high].astype(BF16)
    got_g.append(send(g2.at[1, high], gr2.at[1, high], at_dp(1)))
    got_1a.wait_recv()
    g2[1, low] = (gts[1, low] + gr1[0].astype(F32)).astype(BF16)
    got_g.append(send(g2.at[1, low], gr2.at[1, low], at_dp(1)))
    relay(3)
    gts[0] = target_term(3)
    total = jnp.dot(w[0].reshape(rows, rows), t_ref[...], preferred_element_type=F32)
    for d in range(1, STEPS):
        total += jnp.dot(w[d].reshape(rows, rows), ta[d - 1], preferred_element_type=F32)
    for p in range(NC):
        for i in range(NX * NZ):
            piece = total[half * p + band * i : half * p + band * (i + 1)]
            gq_ref[band * (NC * i + p) : band * (NC * i + p + 1)] = piece * SCALE
    for copy in got_g:
        copy.wait_recv()
    gt_ref[...] = gts[0] + (gr2[0].astype(F32) + gr2[1].astype(F32))
    for copy in started:
        copy.wait_send()


def shards(n_dp, queries, targets, row_lse, col_lse, positive, target_grads):
    rows, cols = queries.shape
    band, half = rows // (NX * NZ * NC), rows // 2
    hbm = pl.BlockSpec(memory_space=pltpu.HBM)
    return pl.pallas_call(
        functools.partial(kernel, n_dp),
        out_shape=(pltpu.VMEM((rows, cols), F32),) * 2,
        in_specs=[hbm] * 6,
        out_specs=(pl.BlockSpec(memory_space=pltpu.VMEM),) * 2,
        scratch_shapes=[
            pltpu.VMEM((rows, cols), BF16),
            pltpu.VMEM((rows, cols), BF16),
            pltpu.VMEM((rows,), F32),
            pltpu.VMEM((rows,), F32),
            pltpu.VMEM((rows,), jnp.int32),
            pltpu.VMEM((rows, cols), F32),
            pltpu.VMEM((NC, half, cols), BF16),
            pltpu.VMEM((half, cols), BF16),
            pltpu.VMEM((STEPS - 1, rows, cols), BF16),
            pltpu.VMEM((STEPS, rows, cols), BF16),
            pltpu.VMEM((rows,), F32),
            pltpu.VMEM((rows,), F32),
            pltpu.VMEM((rows,), F32),
            pltpu.VMEM((STEPS, NX, band * NZ, rows), F32),
            pltpu.VMEM((STEPS, NX, band * NZ, rows), I16),
            pltpu.VMEM((STEPS, NX - 1, band * NZ, rows), I16),
            pltpu.VMEM((STEPS, band * NZ, rows), I16),
            pltpu.VMEM((STEPS, NZ - 1, band * NZ, rows), I16),
            pltpu.VMEM((STEPS, NC, NX, band * NZ, rows), BF16),
            pltpu.VMEM((2, rows, cols), F32),
            pltpu.VMEM((2, half, cols), BF16),
            pltpu.VMEM((2, half, cols), BF16),
            pltpu.VMEM((2, rows, cols), BF16),
            pltpu.VMEM((2, rows, cols), BF16),
            pltpu.SemaphoreType.DMA((LOADS,)),
            pltpu.SemaphoreType.DMA((COPIES,)),
            pltpu.SemaphoreType.DMA((COPIES,)),
        ],
        compiler_params=pltpu.CompilerParams(
            collective_id=0, has_side_effects=True, vmem_limit_bytes=56 << 20
        ),
        cost_estimate=pl.CostEstimate(flops=10**9, bytes_accessed=10**6, transcendentals=10**5),
    )(
        queries, targets, row_lse, col_lse, positive, target_grads
    )


def solution(mesh):
    placed = (P("dp", "tensor"), P("dp", "tensor"), P("dp"), P("dp"), P("dp"), P("dp", "tensor"))
    return jax.shard_map(
        functools.partial(shards, mesh.shape["dp"]),
        mesh=mesh,
        in_specs=placed,
        out_specs=(P("dp", "tensor"), P("dp", "tensor")),
        check_vma=False,
    )
```

```python
import functools
import math

import jax
import jax.numpy as jnp
from jax import lax
from jax.experimental import pallas as pl
from jax.experimental.pallas import tpu as pltpu
from jax.sharding import PartitionSpec as P

D = 3072
STEPS = 4
NX, NZ, NC = 4, 3, 2
SCALE = 2.0 / math.sqrt(D)
COPIES = 80
LOADS = 6
F32 = jnp.float32
BF16 = jnp.bfloat16


def kernel(
    n_dp, q_hbm, t_hbm, rl_hbm, cl_hbm, pos_hbm, tg_hbm, gq_ref, gt_ref,
    q_ref, t_ref, rl_ref, cl_ref, pos_ref, tg_ref,
    qp, qo, ta, tb, cl1, cl2, cl3, sp, xr, zs, zr, w, gts, g1, gr1, g2, gr2, load_sem, send_sem, recv_sem,
):
    rows, cols = q_ref.shape
    band = rows // (NX * NZ * NC)
    xband = band * NZ
    half = rows // 2
    b = lax.axis_index("dp")
    t = lax.axis_index("tensor")
    x, zl, c = t // (NZ * NC), lax.rem(t // NC, NZ), lax.rem(t, NC)

    pairs = ((q_hbm, q_ref), (t_hbm, t_ref), (cl_hbm, cl_ref), (rl_hbm, rl_ref), (pos_hbm, pos_ref), (tg_hbm, tg_ref))
    loads = [pltpu.make_async_copy(src, dst, load_sem.at[i]) for i, (src, dst) in enumerate(pairs)]
    for load in loads:
        load.start()

    def at_dp(k):
        return (lax.rem(b + k + n_dp, n_dp), t)

    def at_x(k):
        return (b, lax.rem(x + k, NX) * (NZ * NC) + zl * NC + c)

    def at_z(k):
        return (b, x * (NZ * NC) + lax.rem(zl + k, NZ) * NC + c)

    mate = (b, t + 1 - 2 * c)

    barrier = pltpu.get_barrier_semaphore()
    partners = [mate] + [at_x(k) for k in (1, 2, 3)] + [at_z(k) for k in (1, 2)]
    partners += [at_dp(k) for k in (1, -1, 2, -2, 3, -3)]
    for dev in partners:
        pl.semaphore_signal(barrier, inc=1, device_id=dev, device_id_type=pl.DeviceIdType.MESH)

    loads[0].wait()
    for i in range(NX * NZ):
        for p in range(NC):
            qp[p, band * i : band * (i + 1)] = q_ref[band * (NC * i + p) : band * (NC * i + p + 1)]
    loads[1].wait()
    loads[2].wait()

    pl.semaphore_wait(barrier, len(partners))

    started = []

    def send(src, dst, dev):
        i = len(started)
        copy = pltpu.make_async_remote_copy(
            src_ref=src, dst_ref=dst, send_sem=send_sem.at[i], recv_sem=recv_sem.at[i],
            device_id=dev, device_id_type=pl.DeviceIdType.MESH,
        )
        copy.start()
        started.append(copy)
        return copy

    cls = (cl1, cl2, cl3)
    own = [t_ref, ta.at[0], ta.at[1], ta.at[2]]
    got_q = send(qp.at[1 - c], qo, mate)
    got_tb = [None] * STEPS
    got_tb[0] = send(t_ref, tb.at[0], mate)
    got_t1 = send(t_ref, ta.at[0], at_dp(1))
    got_t3 = send(t_ref, ta.at[2], at_dp(3))
    got_cl = [None] + [send(cl_ref, cls[k - 1], at_dp(k)) for k in (1, 2, 3)]

    for load in loads[3:]:
        load.wait()
    lane = lax.broadcasted_iota(jnp.int32, (band, rows), 1)
    here = lane == t * band + lax.broadcasted_iota(jnp.int32, (band, rows), 0)
    rl = jnp.sum(jnp.where(here, rl_ref[...].reshape(1, rows), 0.0), axis=1, keepdims=True)
    pos = jnp.sum(jnp.where(here, pos_ref[...].reshape(1, rows), 0), axis=1, keepdims=True)

    got_x, got_z, got_zw, got_xw, got_cw = {}, {}, {}, {}, {}

    def scores(d):
        got_tb[d].wait_recv()
        qq = jnp.concatenate([qp[c], qo[...]], axis=1)
        tt = jnp.concatenate([own[d][...], tb[d]], axis=1)
        s = lax.dot_general(qq, tt, (((1,), (1,)), ((), ())), preferred_element_type=F32)
        sp[d] = s.reshape(NX, xband, rows)
        got_x[d] = [send(sp.at[d, lax.rem(x + k, NX)], xr.at[d, k - 1], at_x(k)) for k in (1, 2, 3)]

    def sum_x(d):
        for copy in got_x[d]:
            copy.wait_recv()
        s = sp[d, x] + xr[d, 0] + xr[d, 1] + xr[d, 2]
        zs[d] = s.reshape(NZ, band, rows)
        got_z[d] = [send(zs.at[d, lax.rem(zl + k, NZ)], zr.at[d, k - 1], at_z(k)) for k in (1, 2)]

    def weigh(d):
        for copy in got_z[d]:
            copy.wait_recv()
        s = (zs[d, zl] + zr[d, 0] + zr[d, 1]) * SCALE
        if d:
            got_cl[d].wait_recv()
        cl = (cls[d - 1] if d else cl_ref)[...].reshape(1, rows)
        match = (pos == lax.rem(b - d + n_dp, n_dp) * rows + lane).astype(F32)
        mine = pl.ds(pl.multiple_of(zl * band, band), band)
        w[d, c, x, mine] = (jnp.exp(s - rl) + jnp.exp(s - cl) - 2.0 * match).astype(BF16)
        got_zw[d] = [send(w.at[d, c, x, mine], w.at[d, c, x, mine], at_z(k)) for k in (1, 2)]

    def gather_x(d):
        for copy in got_zw[d]:
            copy.wait_recv()
        got_xw[d] = [send(w.at[d, c, x], w.at[d, c, x], at_x(k)) for k in (1, 2, 3)]
        got_cw[d] = [send(w.at[d, c, x], w.at[d, c, x], mate)]

    def relay(d):
        for k in (1, 3, 2):
            got_xw[d][k - 1].wait_recv()
            piece = w.at[d, c, lax.rem(x + NX - k, NX)]
            got_cw[d].append(send(piece, piece, mate))

    def gradients(d, first=False):
        for copy in got_cw[d]:
            copy.wait_recv()
        weights = w[d].reshape(rows, rows)
        part = jnp.dot(weights, own[d][...], preferred_element_type=F32) * SCALE
        for p in range(NC):
            for i in range(NX * NZ):
                to = slice(band * (NC * i + p), band * (NC * i + p + 1))
                piece = part[half * p + band * i : half * p + band * (i + 1)]
                gq_ref[to] = piece if first else gq_ref[to] + piece
        queries = qp[...].reshape(rows, cols)
        term = lax.dot_general(weights, queries, (((0,), (0,)), ((), ())), preferred_element_type=F32)
        return term * SCALE

    got_q.wait_recv()
    scores(0)
    sum_x(0)
    got_t1.wait_recv()
    got_t2a = send(ta.at[0, pl.ds(0, half)], ta.at[1, pl.ds(0, half)], at_dp(1))
    got_tb[1] = send(ta.at[0], tb.at[1], mate)
    got_t3.wait_recv()
    got_t2b = send(ta.at[2, pl.ds(half, half)], ta.at[1, pl.ds(half, half)], at_dp(-1))
    got_tb[3] = send(ta.at[2], tb.at[3], mate)
    scores(1)
    weigh(0)
    scores(3)
    sum_x(1)
    gather_x(0)
    sum_x(3)
    got_t2a.wait_recv()
    got_t2b.wait_recv()
    got_tb[2] = send(ta.at[1], tb.at[2], mate)
    weigh(1)
    scores(2)
    relay(0)
    weigh(3)
    gather_x(1)
    sum_x(2)
    gather_x(3)
    relay(1)
    term = gradients(1, first=True)
    g1[...] = term.astype(BF16).reshape(g1.shape)
    got_1a = send(g1.at[0], gr1.at[0], at_dp(1))
    got_1b = send(g1.at[1], gr1.at[1], at_dp(-1))
    weigh(2)
    gts[0] = gradients(0) + tg_ref[...]
    relay(3)
    gather_x(2)
    gts[1] = gradients(3)
    relay(2)
    got_1b.wait_recv()
    g2[0, :half] = gts[0, :half].astype(BF16)
    g2[0, half:] = (gts[0, half:] + gr1[1].astype(F32)).astype(BF16)
    got_20 = send(g2.at[0], gr2.at[0], at_dp(3))
    gts[0] = gradients(2)
    got_1a.wait_recv()
    g2[1, :half] = (gts[0, :half] + gr1[0].astype(F32)).astype(BF16)
    g2[1, half:] = gts[0, half:].astype(BF16)
    got_22 = send(g2.at[1], gr2.at[1], at_dp(1))
    got_20.wait_recv()
    got_22.wait_recv()
    gt_ref[...] = gts[1] + (gr2[0].astype(F32) + gr2[1].astype(F32))
    for copy in started:
        copy.wait_send()


def shards(n_dp, queries, targets, row_lse, col_lse, positive, target_grads):
    rows, cols = queries.shape
    band, half = rows // (NX * NZ * NC), rows // 2
    hbm = pl.BlockSpec(memory_space=pltpu.HBM)
    return pl.pallas_call(
        functools.partial(kernel, n_dp),
        out_shape=(pltpu.VMEM((rows, cols), F32),) * 2,
        in_specs=[hbm] * 6,
        out_specs=(pl.BlockSpec(memory_space=pltpu.VMEM),) * 2,
        scratch_shapes=[
            pltpu.VMEM((rows, cols), BF16),
            pltpu.VMEM((rows, cols), BF16),
            pltpu.VMEM((rows,), F32),
            pltpu.VMEM((rows,), F32),
            pltpu.VMEM((rows,), jnp.int32),
            pltpu.VMEM((rows, cols), F32),
            pltpu.VMEM((NC, half, cols), BF16),
            pltpu.VMEM((half, cols), BF16),
            pltpu.VMEM((STEPS - 1, rows, cols), BF16),
            pltpu.VMEM((STEPS, rows, cols), BF16),
            pltpu.VMEM((rows,), F32),
            pltpu.VMEM((rows,), F32),
            pltpu.VMEM((rows,), F32),
            pltpu.VMEM((STEPS, NX, band * NZ, rows), F32),
            pltpu.VMEM((STEPS, NX - 1, band * NZ, rows), F32),
            pltpu.VMEM((STEPS, NZ, band, rows), F32),
            pltpu.VMEM((STEPS, NZ - 1, band, rows), F32),
            pltpu.VMEM((STEPS, NC, NX, band * NZ, rows), BF16),
            pltpu.VMEM((2, rows, cols), F32),
            pltpu.VMEM((2, half, cols), BF16),
            pltpu.VMEM((2, half, cols), BF16),
            pltpu.VMEM((2, rows, cols), BF16),
            pltpu.VMEM((2, rows, cols), BF16),
            pltpu.SemaphoreType.DMA((LOADS,)),
            pltpu.SemaphoreType.DMA((COPIES,)),
            pltpu.SemaphoreType.DMA((COPIES,)),
        ],
        compiler_params=pltpu.CompilerParams(
            collective_id=0, has_side_effects=True, vmem_limit_bytes=56 << 20
        ),
        cost_estimate=pl.CostEstimate(flops=10**9, bytes_accessed=10**6, transcendentals=10**5),
    )(
        queries, targets, row_lse, col_lse, positive, target_grads
    )


def solution(mesh):
    placed = (P("dp", "tensor"), P("dp", "tensor"), P("dp"), P("dp"), P("dp"), P("dp", "tensor"))
    return jax.shard_map(
        functools.partial(shards, mesh.shape["dp"]),
        mesh=mesh,
        in_specs=placed,
        out_specs=(P("dp", "tensor"), P("dp", "tensor")),
        check_vma=False,
    )
```

```python
import functools
import math

import jax
import jax.numpy as jnp
from jax import lax
from jax.experimental import pallas as pl
from jax.experimental.pallas import tpu as pltpu
from jax.sharding import PartitionSpec as P

D = 3072
STEPS = 4
NX, NZ, NC = 4, 3, 2
SCALE = 2.0 / math.sqrt(D)
COPIES = 80
LOADS = 6
F32 = jnp.float32
BF16 = jnp.bfloat16


def kernel(
    n_dp, q_hbm, t_hbm, rl_hbm, cl_hbm, pos_hbm, tg_hbm, gq_ref, gt_ref,
    q_ref, t_ref, rl_ref, cl_ref, pos_ref, tg_ref,
    qp, qo, ta, tb, cl1, cl2, cl3, sp, xr, zs, zr, w, gts, g1, gr1, g2, gr2, load_sem, send_sem, recv_sem,
):
    rows, cols = q_ref.shape
    band = rows // (NX * NZ * NC)
    xband = band * NZ
    half = rows // 2
    b = lax.axis_index("dp")
    t = lax.axis_index("tensor")
    x, zl, c = t // (NZ * NC), lax.rem(t // NC, NZ), lax.rem(t, NC)

    pairs = ((q_hbm, q_ref), (t_hbm, t_ref), (cl_hbm, cl_ref), (rl_hbm, rl_ref), (pos_hbm, pos_ref), (tg_hbm, tg_ref))
    loads = [pltpu.make_async_copy(src, dst, load_sem.at[i]) for i, (src, dst) in enumerate(pairs)]
    for load in loads:
        load.start()

    def at_dp(k):
        return (lax.rem(b + k + n_dp, n_dp), t)

    def at_x(k):
        return (b, lax.rem(x + k, NX) * (NZ * NC) + zl * NC + c)

    def at_z(k):
        return (b, x * (NZ * NC) + lax.rem(zl + k, NZ) * NC + c)

    mate = (b, t + 1 - 2 * c)

    barrier = pltpu.get_barrier_semaphore()
    partners = [mate] + [at_x(k) for k in (1, 2, 3)] + [at_z(k) for k in (1, 2)]
    partners += [at_dp(k) for k in (1, -1, 2, -2, 3, -3)]
    for dev in partners:
        pl.semaphore_signal(barrier, inc=1, device_id=dev, device_id_type=pl.DeviceIdType.MESH)

    loads[0].wait()
    for i in range(NX * NZ):
        for p in range(NC):
            qp[p, band * i : band * (i + 1)] = q_ref[band * (NC * i + p) : band * (NC * i + p + 1)]
    loads[1].wait()
    loads[2].wait()

    pl.semaphore_wait(barrier, len(partners))

    started = []

    def send(src, dst, dev):
        i = len(started)
        copy = pltpu.make_async_remote_copy(
            src_ref=src, dst_ref=dst, send_sem=send_sem.at[i], recv_sem=recv_sem.at[i],
            device_id=dev, device_id_type=pl.DeviceIdType.MESH,
        )
        copy.start()
        started.append(copy)
        return copy

    cls = (cl1, cl2, cl3)
    own = [t_ref, ta.at[0], ta.at[1], ta.at[2]]
    got_q = send(qp.at[1 - c], qo, mate)
    got_tb = [None] * STEPS
    got_tb[0] = send(t_ref, tb.at[0], mate)
    got_t1 = send(t_ref, ta.at[0], at_dp(1))
    got_t3 = send(t_ref, ta.at[2], at_dp(3))
    got_cl = [None] + [send(cl_ref, cls[k - 1], at_dp(k)) for k in (1, 2, 3)]

    for load in loads[3:]:
        load.wait()
    lane = lax.broadcasted_iota(jnp.int32, (band, rows), 1)
    here = lane == t * band + lax.broadcasted_iota(jnp.int32, (band, rows), 0)
    rl = jnp.sum(jnp.where(here, rl_ref[...].reshape(1, rows), 0.0), axis=1, keepdims=True)
    pos = jnp.sum(jnp.where(here, pos_ref[...].reshape(1, rows), 0), axis=1, keepdims=True)

    got_x, got_z, got_zw, got_xw, got_cw = {}, {}, {}, {}, {}

    def scores(d):
        got_tb[d].wait_recv()
        qq = jnp.concatenate([qp[c], qo[...]], axis=1)
        tt = jnp.concatenate([own[d][...], tb[d]], axis=1)
        s = lax.dot_general(qq, tt, (((1,), (1,)), ((), ())), preferred_element_type=F32)
        sp[d] = s.reshape(NX, xband, rows)
        got_x[d] = [send(sp.at[d, lax.rem(x + k, NX)], xr.at[d, k - 1], at_x(k)) for k in (1, 2, 3)]

    def sum_x(d):
        for copy in got_x[d]:
            copy.wait_recv()
        s = sp[d, x] + xr[d, 0] + xr[d, 1] + xr[d, 2]
        zs[d] = s.reshape(NZ, band, rows)
        got_z[d] = [send(zs.at[d, lax.rem(zl + k, NZ)], zr.at[d, k - 1], at_z(k)) for k in (1, 2)]

    def weigh(d):
        for copy in got_z[d]:
            copy.wait_recv()
        s = (zs[d, zl] + zr[d, 0] + zr[d, 1]) * SCALE
        if d:
            got_cl[d].wait_recv()
        cl = (cls[d - 1] if d else cl_ref)[...].reshape(1, rows)
        match = (pos == lax.rem(b - d + n_dp, n_dp) * rows + lane).astype(F32)
        mine = pl.ds(pl.multiple_of(zl * band, band), band)
        w[d, c, x, mine] = (jnp.exp(s - rl) + jnp.exp(s - cl) - 2.0 * match).astype(BF16)
        got_zw[d] = [send(w.at[d, c, x, mine], w.at[d, c, x, mine], at_z(k)) for k in (1, 2)]

    def gather_x(d):
        for copy in got_zw[d]:
            copy.wait_recv()
        got_xw[d] = [send(w.at[d, c, x], w.at[d, c, x], at_x(k)) for k in (1, 2, 3)]
        got_cw[d] = [send(w.at[d, c, x], w.at[d, c, x], mate)]

    def relay(d):
        for k in (1, 3, 2):
            got_xw[d][k - 1].wait_recv()
            piece = w.at[d, c, lax.rem(x + NX - k, NX)]
            got_cw[d].append(send(piece, piece, mate))

    def gradients(d, first=False):
        for copy in got_cw[d]:
            copy.wait_recv()
        weights = w[d].reshape(rows, rows)
        part = jnp.dot(weights, own[d][...], preferred_element_type=F32) * SCALE
        for p in range(NC):
            for i in range(NX * NZ):
                to = slice(band * (NC * i + p), band * (NC * i + p + 1))
                piece = part[half * p + band * i : half * p + band * (i + 1)]
                gq_ref[to] = piece if first else gq_ref[to] + piece
        queries = qp[...].reshape(rows, cols)
        term = lax.dot_general(weights, queries, (((0,), (0,)), ((), ())), preferred_element_type=F32)
        return term * SCALE

    got_q.wait_recv()
    scores(0)
    sum_x(0)
    got_t1.wait_recv()
    got_t2a = send(ta.at[0, pl.ds(0, half)], ta.at[1, pl.ds(0, half)], at_dp(1))
    got_tb[1] = send(ta.at[0], tb.at[1], mate)
    got_t3.wait_recv()
    got_t2b = send(ta.at[2, pl.ds(half, half)], ta.at[1, pl.ds(half, half)], at_dp(-1))
    got_tb[3] = send(ta.at[2], tb.at[3], mate)
    scores(1)
    weigh(0)
    scores(3)
    sum_x(1)
    gather_x(0)
    got_t2a.wait_recv()
    got_t2b.wait_recv()
    got_tb[2] = send(ta.at[1], tb.at[2], mate)
    sum_x(3)
    weigh(1)
    scores(2)
    relay(0)
    gather_x(1)
    weigh(3)
    sum_x(2)
    gather_x(3)
    relay(1)
    weigh(2)
    term = gradients(1, first=True)
    g1[...] = term.astype(BF16).reshape(g1.shape)
    got_1a = send(g1.at[0], gr1.at[0], at_dp(1))
    got_1b = send(g1.at[1], gr1.at[1], at_dp(-1))
    gts[0] = gradients(0) + tg_ref[...]
    relay(3)
    gather_x(2)
    gts[1] = gradients(3)
    relay(2)
    got_1b.wait_recv()
    g2[0, :half] = gts[0, :half].astype(BF16)
    g2[0, half:] = (gts[0, half:] + gr1[1].astype(F32)).astype(BF16)
    got_20 = send(g2.at[0], gr2.at[0], at_dp(3))
    gts[0] = gradients(2)
    got_1a.wait_recv()
    g2[1, :half] = (gts[0, :half] + gr1[0].astype(F32)).astype(BF16)
    g2[1, half:] = gts[0, half:].astype(BF16)
    got_22 = send(g2.at[1], gr2.at[1], at_dp(1))
    got_20.wait_recv()
    got_22.wait_recv()
    gt_ref[...] = gts[1] + (gr2[0].astype(F32) + gr2[1].astype(F32))
    for copy in started:
        copy.wait_send()


def shards(n_dp, queries, targets, row_lse, col_lse, positive, target_grads):
    rows, cols = queries.shape
    band, half = rows // (NX * NZ * NC), rows // 2
    hbm = pl.BlockSpec(memory_space=pltpu.HBM)
    return pl.pallas_call(
        functools.partial(kernel, n_dp),
        out_shape=(pltpu.VMEM((rows, cols), F32),) * 2,
        in_specs=[hbm] * 6,
        out_specs=(pl.BlockSpec(memory_space=pltpu.VMEM),) * 2,
        scratch_shapes=[
            pltpu.VMEM((rows, cols), BF16),
            pltpu.VMEM((rows, cols), BF16),
            pltpu.VMEM((rows,), F32),
            pltpu.VMEM((rows,), F32),
            pltpu.VMEM((rows,), jnp.int32),
            pltpu.VMEM((rows, cols), F32),
            pltpu.VMEM((NC, half, cols), BF16),
            pltpu.VMEM((half, cols), BF16),
            pltpu.VMEM((STEPS - 1, rows, cols), BF16),
            pltpu.VMEM((STEPS, rows, cols), BF16),
            pltpu.VMEM((rows,), F32),
            pltpu.VMEM((rows,), F32),
            pltpu.VMEM((rows,), F32),
            pltpu.VMEM((STEPS, NX, band * NZ, rows), F32),
            pltpu.VMEM((STEPS, NX - 1, band * NZ, rows), F32),
            pltpu.VMEM((STEPS, NZ, band, rows), F32),
            pltpu.VMEM((STEPS, NZ - 1, band, rows), F32),
            pltpu.VMEM((STEPS, NC, NX, band * NZ, rows), BF16),
            pltpu.VMEM((2, rows, cols), F32),
            pltpu.VMEM((2, half, cols), BF16),
            pltpu.VMEM((2, half, cols), BF16),
            pltpu.VMEM((2, rows, cols), BF16),
            pltpu.VMEM((2, rows, cols), BF16),
            pltpu.SemaphoreType.DMA((LOADS,)),
            pltpu.SemaphoreType.DMA((COPIES,)),
            pltpu.SemaphoreType.DMA((COPIES,)),
        ],
        compiler_params=pltpu.CompilerParams(
            collective_id=0, has_side_effects=True, vmem_limit_bytes=56 << 20
        ),
        cost_estimate=pl.CostEstimate(flops=10**9, bytes_accessed=10**6, transcendentals=10**5),
    )(
        queries, targets, row_lse, col_lse, positive, target_grads
    )


def solution(mesh):
    placed = (P("dp", "tensor"), P("dp", "tensor"), P("dp"), P("dp"), P("dp"), P("dp", "tensor"))
    return jax.shard_map(
        functools.partial(shards, mesh.shape["dp"]),
        mesh=mesh,
        in_specs=placed,
        out_specs=(P("dp", "tensor"), P("dp", "tensor")),
        check_vma=False,
    )
```

```python
import functools
import math

import jax
import jax.numpy as jnp
from jax import lax
from jax.experimental import pallas as pl
from jax.experimental.pallas import tpu as pltpu
from jax.sharding import PartitionSpec as P

D = 3072
STEPS = 4
NX, NZ, NC = 4, 3, 2
SCALE = 2.0 / math.sqrt(D)
COPIES = 80
LOADS = 6
F32 = jnp.float32
BF16 = jnp.bfloat16


def kernel(
    n_dp, q_hbm, t_hbm, rl_hbm, cl_hbm, pos_hbm, tg_hbm, gq_ref, gt_ref,
    q_ref, t_ref, rl_ref, cl_ref, pos_ref, tg_ref,
    qp, qo, ta, tb, cl1, cl2, cl3, sp, xr, zs, zr, w, gts, g1, gr1, g2, gr2, load_sem, send_sem, recv_sem,
):
    rows, cols = q_ref.shape
    band = rows // (NX * NZ * NC)
    xband = band * NZ
    half = rows // 2
    b = lax.axis_index("dp")
    t = lax.axis_index("tensor")
    x, zl, c = t // (NZ * NC), lax.rem(t // NC, NZ), lax.rem(t, NC)

    pairs = ((q_hbm, q_ref), (t_hbm, t_ref), (cl_hbm, cl_ref), (rl_hbm, rl_ref), (pos_hbm, pos_ref), (tg_hbm, tg_ref))
    loads = [pltpu.make_async_copy(src, dst, load_sem.at[i]) for i, (src, dst) in enumerate(pairs)]
    for load in loads:
        load.start()

    def at_dp(k):
        return (lax.rem(b + k + n_dp, n_dp), t)

    def at_x(k):
        return (b, lax.rem(x + k, NX) * (NZ * NC) + zl * NC + c)

    def at_z(k):
        return (b, x * (NZ * NC) + lax.rem(zl + k, NZ) * NC + c)

    mate = (b, t + 1 - 2 * c)

    barrier = pltpu.get_barrier_semaphore()
    partners = [mate] + [at_x(k) for k in (1, 2, 3)] + [at_z(k) for k in (1, 2)]
    partners += [at_dp(k) for k in (1, -1, 2, -2, 3, -3)]
    for dev in partners:
        pl.semaphore_signal(barrier, inc=1, device_id=dev, device_id_type=pl.DeviceIdType.MESH)

    loads[0].wait()
    for i in range(NX * NZ):
        for p in range(NC):
            qp[p, band * i : band * (i + 1)] = q_ref[band * (NC * i + p) : band * (NC * i + p + 1)]
    loads[1].wait()
    loads[2].wait()

    pl.semaphore_wait(barrier, len(partners))

    started = []

    def send(src, dst, dev):
        i = len(started)
        copy = pltpu.make_async_remote_copy(
            src_ref=src, dst_ref=dst, send_sem=send_sem.at[i], recv_sem=recv_sem.at[i],
            device_id=dev, device_id_type=pl.DeviceIdType.MESH,
        )
        copy.start()
        started.append(copy)
        return copy

    cls = (cl1, cl2, cl3)
    own = [t_ref, ta.at[0], ta.at[1], ta.at[2]]
    got_q = send(qp.at[1 - c], qo, mate)
    got_tb = [None] * STEPS
    got_tb[0] = send(t_ref, tb.at[0], mate)
    got_t1 = send(t_ref, ta.at[0], at_dp(1))
    got_t3 = send(t_ref, ta.at[2], at_dp(3))
    got_cl = [None] + [send(cl_ref, cls[k - 1], at_dp(k)) for k in (1, 2, 3)]

    for load in loads[3:]:
        load.wait()
    lane = lax.broadcasted_iota(jnp.int32, (band, rows), 1)
    here = lane == t * band + lax.broadcasted_iota(jnp.int32, (band, rows), 0)
    rl = jnp.sum(jnp.where(here, rl_ref[...].reshape(1, rows), 0.0), axis=1, keepdims=True)
    pos = jnp.sum(jnp.where(here, pos_ref[...].reshape(1, rows), 0), axis=1, keepdims=True)

    got_x, got_z, got_zw, got_xw, got_cw = {}, {}, {}, {}, {}

    def scores(d):
        got_tb[d].wait_recv()
        qq = jnp.concatenate([qp[c], qo[...]], axis=1)
        tt = jnp.concatenate([own[d][...], tb[d]], axis=1)
        s = lax.dot_general(qq, tt, (((1,), (1,)), ((), ())), preferred_element_type=F32)
        sp[d] = s.reshape(NX, xband, rows)
        got_x[d] = [send(sp.at[d, lax.rem(x + k, NX)], xr.at[d, k - 1], at_x(k)) for k in (1, 2, 3)]

    def sum_x(d):
        for copy in got_x[d]:
            copy.wait_recv()
        s = sp[d, x] + xr[d, 0] + xr[d, 1] + xr[d, 2]
        zs[d] = s.reshape(NZ, band, rows)
        got_z[d] = [send(zs.at[d, lax.rem(zl + k, NZ)], zr.at[d, k - 1], at_z(k)) for k in (1, 2)]

    def weigh(d):
        for copy in got_z[d]:
            copy.wait_recv()
        s = (zs[d, zl] + zr[d, 0] + zr[d, 1]) * SCALE
        if d:
            got_cl[d].wait_recv()
        cl = (cls[d - 1] if d else cl_ref)[...].reshape(1, rows)
        match = (pos == lax.rem(b - d + n_dp, n_dp) * rows + lane).astype(F32)
        mine = pl.ds(pl.multiple_of(zl * band, band), band)
        w[d, c, x, mine] = (jnp.exp(s - rl) + jnp.exp(s - cl) - 2.0 * match).astype(BF16)
        got_zw[d] = [send(w.at[d, c, x, mine], w.at[d, c, x, mine], at_z(k)) for k in (1, 2)]

    def gather_x(d):
        for copy in got_zw[d]:
            copy.wait_recv()
        got_xw[d] = [send(w.at[d, c, x], w.at[d, c, x], at_x(k)) for k in (1, 2, 3)]
        got_cw[d] = [send(w.at[d, c, x], w.at[d, c, x], mate)]

    def relay(d):
        for k in (1, 3, 2):
            got_xw[d][k - 1].wait_recv()
            piece = w.at[d, c, lax.rem(x + NX - k, NX)]
            got_cw[d].append(send(piece, piece, mate))

    def gradients(d, first=False):
        for copy in got_cw[d]:
            copy.wait_recv()
        weights = w[d].reshape(rows, rows)
        part = jnp.dot(weights, own[d][...], preferred_element_type=F32) * SCALE
        for p in range(NC):
            for i in range(NX * NZ):
                to = slice(band * (NC * i + p), band * (NC * i + p + 1))
                piece = part[half * p + band * i : half * p + band * (i + 1)]
                gq_ref[to] = piece if first else gq_ref[to] + piece
        queries = qp[...].reshape(rows, cols)
        term = lax.dot_general(weights, queries, (((0,), (0,)), ((), ())), preferred_element_type=F32)
        return term * SCALE

    got_q.wait_recv()
    scores(0)
    sum_x(0)
    got_t1.wait_recv()
    got_t2a = send(ta.at[0, pl.ds(0, half)], ta.at[1, pl.ds(0, half)], at_dp(1))
    got_tb[1] = send(ta.at[0], tb.at[1], mate)
    got_t3.wait_recv()
    got_t2b = send(ta.at[2, pl.ds(half, half)], ta.at[1, pl.ds(half, half)], at_dp(-1))
    got_tb[3] = send(ta.at[2], tb.at[3], mate)
    scores(1)
    weigh(0)
    scores(3)
    sum_x(1)
    gather_x(0)
    got_t2a.wait_recv()
    got_t2b.wait_recv()
    got_tb[2] = send(ta.at[1], tb.at[2], mate)
    sum_x(3)
    scores(2)
    weigh(1)
    relay(0)
    gather_x(1)
    weigh(3)
    sum_x(2)
    gather_x(3)
    relay(1)
    weigh(2)
    term = gradients(1, first=True)
    g1[...] = term.astype(BF16).reshape(g1.shape)
    got_1a = send(g1.at[0], gr1.at[0], at_dp(1))
    got_1b = send(g1.at[1], gr1.at[1], at_dp(-1))
    relay(3)
    gather_x(2)
    gts[0] = gradients(0) + tg_ref[...]
    relay(2)
    got_1b.wait_recv()
    g2[0, :half] = gts[0, :half].astype(BF16)
    g2[0, half:] = (gts[0, half:] + gr1[1].astype(F32)).astype(BF16)
    got_20 = send(g2.at[0], gr2.at[0], at_dp(3))
    gts[0] = gradients(2)
    got_1a.wait_recv()
    g2[1, :half] = (gts[0, :half] + gr1[0].astype(F32)).astype(BF16)
    g2[1, half:] = gts[0, half:].astype(BF16)
    got_22 = send(g2.at[1], gr2.at[1], at_dp(1))
    gts[1] = gradients(3)
    got_20.wait_recv()
    got_22.wait_recv()
    gt_ref[...] = gts[1] + (gr2[0].astype(F32) + gr2[1].astype(F32))
    for copy in started:
        copy.wait_send()


def shards(n_dp, queries, targets, row_lse, col_lse, positive, target_grads):
    rows, cols = queries.shape
    band, half = rows // (NX * NZ * NC), rows // 2
    hbm = pl.BlockSpec(memory_space=pltpu.HBM)
    return pl.pallas_call(
        functools.partial(kernel, n_dp),
        out_shape=(pltpu.VMEM((rows, cols), F32),) * 2,
        in_specs=[hbm] * 6,
        out_specs=(pl.BlockSpec(memory_space=pltpu.VMEM),) * 2,
        scratch_shapes=[
            pltpu.VMEM((rows, cols), BF16),
            pltpu.VMEM((rows, cols), BF16),
            pltpu.VMEM((rows,), F32),
            pltpu.VMEM((rows,), F32),
            pltpu.VMEM((rows,), jnp.int32),
            pltpu.VMEM((rows, cols), F32),
            pltpu.VMEM((NC, half, cols), BF16),
            pltpu.VMEM((half, cols), BF16),
            pltpu.VMEM((STEPS - 1, rows, cols), BF16),
            pltpu.VMEM((STEPS, rows, cols), BF16),
            pltpu.VMEM((rows,), F32),
            pltpu.VMEM((rows,), F32),
            pltpu.VMEM((rows,), F32),
            pltpu.VMEM((STEPS, NX, band * NZ, rows), F32),
            pltpu.VMEM((STEPS, NX - 1, band * NZ, rows), F32),
            pltpu.VMEM((STEPS, NZ, band, rows), F32),
            pltpu.VMEM((STEPS, NZ - 1, band, rows), F32),
            pltpu.VMEM((STEPS, NC, NX, band * NZ, rows), BF16),
            pltpu.VMEM((2, rows, cols), F32),
            pltpu.VMEM((2, half, cols), BF16),
            pltpu.VMEM((2, half, cols), BF16),
            pltpu.VMEM((2, rows, cols), BF16),
            pltpu.VMEM((2, rows, cols), BF16),
            pltpu.SemaphoreType.DMA((LOADS,)),
            pltpu.SemaphoreType.DMA((COPIES,)),
            pltpu.SemaphoreType.DMA((COPIES,)),
        ],
        compiler_params=pltpu.CompilerParams(
            collective_id=0, has_side_effects=True, vmem_limit_bytes=56 << 20
        ),
        cost_estimate=pl.CostEstimate(flops=10**9, bytes_accessed=10**6, transcendentals=10**5),
    )(
        queries, targets, row_lse, col_lse, positive, target_grads
    )


def solution(mesh):
    placed = (P("dp", "tensor"), P("dp", "tensor"), P("dp"), P("dp"), P("dp"), P("dp", "tensor"))
    return jax.shard_map(
        functools.partial(shards, mesh.shape["dp"]),
        mesh=mesh,
        in_specs=placed,
        out_specs=(P("dp", "tensor"), P("dp", "tensor")),
        check_vma=False,
    )
```
